32 devices in a mesh: gx: 4 (over z), gy: 2 (over y), gz: 4 (over x, core).
Axes of the slice: x: 2, y: 2, z: 4, core: 2. Of those that a mesh axis runs over, the one named last changes fastest.
Arguments:
- checkpoint: float32 [19, 64, 32, 512], P(None, 'gx', 'gy', 'gz'), may hold values from 0.005 to 0.6, as said below
- adjoint: float32 [19, 64, 32, 512], P(None, 'gx', 'gy', 'gz'), may hold values from -6 to 6
- porosity: float32 [64, 32, 512], P('gx', 'gy', 'gz'), may hold values from 0 to 0.5
- solid: int32 [64, 32, 512], P('gx', 'gy', 'gz'), may hold values 0 or 1
- gradient_in: float32 [64, 32, 512], P('gx', 'gy', 'gz'), may hold values from -6 to 6
Outputs:
- adjoint_out: float32 [19, 64, 32, 512], P(None, 'gx', 'gy', 'gz')
- gradient_out: float32 [64, 32, 512], P('gx', 'gy', 'gz')
The draws below stay inside these ranges and needn't reach their ends.
Inputs may be any that keep to these rules, and one draw needn't show every extreme that they name: `checkpoint`: each population is positive and near w_i times a density of order one.
All inputs are finite; a program needn't handle non-finite values. No bound on the sum of `solid` on one device may be relied on, other than what follows from the above.
Results may differ from the reference program's by a relative error of at most 0.0001.
Values sent between devices are 32-bit elements; how exact they have to be, the bound alone decides.
A program may use at most 128 MiB of HBM per device.

```python
import jax
import jax.numpy as jnp
from jax import lax

RECOMP = 3
NX = 64
NY = 32
NZ = 512


def draw_checkpoint(key, part):
    key = jax.random.fold_in(key, 1)
    weights = jnp.array([1.0 / 3.0] + [1.0 / 18.0] * 6 + [1.0 / 36.0] * 12, jnp.float32).reshape(19, 1, 1, 1)
    second = jax.random.fold_in(key, 1)
    noise = jax.random.uniform(second, (19, NX, NY, NZ), jnp.float32, 0.7, 1.3)
    return weights * noise


def plant(values, rng, least, largest):
    shape = values.shape
    index_at = [jax.random.randint(jax.random.fold_in(rng, axis), (), 0, shape[axis]) for axis in range(len(shape))]
    values = values.at[tuple(index_at)].set(least)
    longest = shape.index(max(shape))
    index_at[longest] = (index_at[longest] + 1) % shape[longest]
    return values.at[tuple(index_at)].set(largest)


def block_levels(rng, dims, cuts, least, largest):
    loudness = 1.0
    for axis_at, parts in cuts:
        draws = jax.random.uniform(jax.random.fold_in(jax.random.fold_in(rng, 6), axis_at), (parts,), jnp.float32, least / len(cuts), largest / len(cuts))
        loudness = loudness * jnp.repeat(jnp.exp(draws), dims[axis_at] // parts).reshape((-1,) + (1,) * (len(dims) - 1 - axis_at))
    return loudness


def centred(key, extent, spread, reach, cuts=(), kind=jnp.bfloat16):
    values = spread * jax.random.normal(key, extent, jnp.float32)
    if cuts:
        values = values * block_levels(key, extent, cuts, -0.22, 0.18)
    return jnp.clip(values, -reach, reach).astype(kind)


def setup_inputs(seed: int = 0) -> dict:
    streams_of = jax.random.split(jax.random.key(seed), 6)
    checkpoint = draw_checkpoint(jax.random.fold_in(streams_of[5], 71), 0)
    adjoint = centred(streams_of[1], (19, NX, NY, NZ), 1.0, 6.0, ((1, 4), (2, 2), (3, 4)), jnp.float32)
    porosity = jnp.clip(0.5 * jax.random.uniform(streams_of[2], (NX, NY, NZ), jnp.float32) ** block_levels(streams_of[2], (NX, NY, NZ), ((0, 4), (1, 2), (2, 4)), -0.2, 0.2), 0.0, 0.5)
    solid = plant((jax.random.randint(streams_of[3], (NX, NY, NZ), 0, 4) < 1).astype(jnp.int32), jax.random.fold_in(streams_of[3], 1), 0, 1)
    gradient_in = centred(streams_of[4], (NX, NY, NZ), 1.0, 6.0, ((0, 4), (1, 2), (2, 4)), jnp.float32)
    return dict(checkpoint=checkpoint, adjoint=adjoint, porosity=porosity, solid=solid, gradient_in=gradient_in)


VELOCITIES = [(0, 0, 0), (1, 0, 0), (-1, 0, 0), (0, 1, 0), (0, -1, 0), (0, 0, 1), (0, 0, -1), (1, 1, 0), (-1, -1, 0), (1, -1, 0), (-1, 1, 0), (1, 0, 1), (-1, 0, -1), (1, 0, -1), (-1, 0, 1), (0, 1, 1), (0, -1, -1), (0, 1, -1), (0, -1, 1)]
OPPOSITE = [0, 2, 1, 4, 3, 6, 5, 8, 7, 10, 9, 12, 11, 14, 13, 16, 15, 18, 17]
WEIGHTS = [1.0 / 3.0] + [1.0 / 18.0] * 6 + [1.0 / 36.0] * 12
RELAX = 1.25

def collide(fields, gamma):
    shaped = (19,) + (1,) * (fields.ndim - 1)
    weights = jnp.array(WEIGHTS, fields.dtype).reshape(shaped)
    table = jnp.array(VELOCITIES, fields.dtype)
    vel_x = table[:, 0].reshape(shaped)
    vel_y = table[:, 1].reshape(shaped)
    vel_z = table[:, 2].reshape(shaped)
    density = lax.optimization_barrier(jnp.sum(fields, 0))
    speed_x = lax.optimization_barrier(jnp.sum(vel_x * fields, 0)) / density
    speed_y = lax.optimization_barrier(jnp.sum(vel_y * fields, 0)) / density
    speed_z = lax.optimization_barrier(jnp.sum(vel_z * fields, 0)) / density
    projected = vel_x * speed_x + vel_y * speed_y + vel_z * speed_z
    squared = speed_x * speed_x + speed_y * speed_y + speed_z * speed_z
    equilibrium = weights * density * (1.0 + 3.0 * projected + 4.5 * projected * projected - 1.5 * squared)
    relaxed = fields - RELAX * (fields - equilibrium)
    bounced = jnp.stack([fields[other] for other in OPPOSITE], 0)
    return ((1.0 - gamma) * relaxed + gamma * bounced, relaxed, bounced)

def reference(checkpoint, adjoint, porosity, solid, gradient_in):
    gamma = jnp.where(solid == 1, jnp.ones_like(porosity), porosity)
    fields = checkpoint
    for step in range(RECOMP):
        post = collide(fields, gamma)[0]
        fields = jnp.stack([jnp.roll(post[number], VELOCITIES[number], (0, 1, 2)) for number in range(19)], 0)
    pulled = jnp.stack([jnp.roll(adjoint[number], tuple((-v for v in VELOCITIES[number])), (0, 1, 2)) for number in range(19)], 0)
    _, relaxed, bounced = collide(fields, gamma)
    _, backward = jax.vjp(lambda values: collide(values, gamma)[0], fields)
    adjoint_out = backward(pulled)[0]
    pore = 1.0 - solid.astype(porosity.dtype)
    gradient_out = gradient_in + pore * lax.optimization_barrier(jnp.sum(pulled * (bounced - relaxed), 0))
    return (adjoint_out, gradient_out)
```

```python
import functools

import jax
import jax.numpy as jnp
from jax import lax
from jax.experimental import pallas as pl
from jax.experimental.pallas import tpu as pltpu
from jax.sharding import PartitionSpec as P

RECOMP = 3
VELOCITIES = [
    (0, 0, 0),
    (1, 0, 0),
    (-1, 0, 0),
    (0, 1, 0),
    (0, -1, 0),
    (0, 0, 1),
    (0, 0, -1),
    (1, 1, 0),
    (-1, -1, 0),
    (1, -1, 0),
    (-1, 1, 0),
    (1, 0, 1),
    (-1, 0, -1),
    (1, 0, -1),
    (-1, 0, 1),
    (0, 1, 1),
    (0, -1, -1),
    (0, 1, -1),
    (0, -1, 1),
]
OPPOSITE = [0, 2, 1, 4, 3, 6, 5, 8, 7, 10, 9, 12, 11, 14, 13, 16, 15, 18, 17]
PAIRS = [(1, 2), (3, 4), (5, 6), (7, 8), (9, 10), (11, 12), (13, 14), (15, 16), (17, 18)]
WEIGHTS = [1.0 / 3.0] + [1.0 / 18.0] * 6 + [1.0 / 36.0] * 12
RELAX = 1.25

ORDER = [1, 7, 9, 11, 13, 2, 8, 10, 12, 14, 0, 3, 4, 5, 6, 15, 16, 17, 18]
SLOT = [ORDER.index(i) for i in range(19)]
Y_GROUP = [[i for i in range(19) if VELOCITIES[i][1] == s] for s in (1, -1)]
Z_GROUP = [[i for i in range(19) if VELOCITIES[i][2] == s] for s in (1, -1)]
AXES = ("gx", "gy", "gz")
ADJ = RECOMP
ROUNDS = RECOMP + 1
MESH_ID = pl.DeviceIdType.MESH


def side(component):
    return 0 if component > 0 else 1


def moments(f):
    plus = [f[i] + f[o] for i, o in PAIRS]
    minus = [f[i] - f[o] for i, o in PAIRS]
    rho = f[0]
    for s in plus:
        rho = rho + s
    flow = []
    for axis in range(3):
        total = None
        for (i, _), d in zip(PAIRS, minus):
            c = VELOCITIES[i][axis]
            if c == 0:
                continue
            total = d if total is None else (total + d if c > 0 else total - d)
        flow.append(total)
    return rho, flow


def along(vector, i):
    total = None
    for axis in range(3):
        c = VELOCITIES[i][axis]
        if c == 0:
            continue
        if total is None:
            total = vector[axis] if c > 0 else -vector[axis]
        else:
            total = total + vector[axis] if c > 0 else total - vector[axis]
    return total


def collide(f, gamma):
    rho, flow = moments(f)
    inv = 1.0 / rho
    u = [j * inv for j in flow]
    fluid = 1.0 - gamma
    keep = (1.0 - RELAX) * fluid
    gain = RELAX * fluid
    scaled = gain * rho
    squared = u[0] * u[0] + u[1] * u[1] + u[2] * u[2]
    base = scaled - 1.5 * scaled * squared
    triple = (3.0 / 36.0) * scaled
    base_edge = (1.0 / 36.0) * base
    base_face = base_edge + base_edge
    post = [None] * 19
    post[0] = (keep + gamma) * f[0] + (1.0 / 3.0) * base
    for i, o in PAIRS:
        q = along(u, i)
        t = triple * q
        even = 1.5 * q * t
        if i < 7:
            t = t + t
            even = even + even + base_face
        else:
            even = even + base_edge
        post[i] = keep * f[i] + gamma * f[o] + (even + t)
        post[o] = keep * f[o] + gamma * f[i] + (even - t)
    return post


def kernel(nx, ny, nz, chunk, ck_hbm, adj_hbm, por_hbm, sol_hbm, gin_hbm, out_hbm, grad_hbm,
           ck, post, ystage, yhalo, zstage, zrecv, zmerge, base, coef, gsum, por, sol, gin,
           outv, gradv, send_sem, recv_sem, ck_sem, adj_sem, small_sem, out_sem):
    sizes = [lax.axis_size(a) for a in AXES]
    me = [lax.axis_index(a) for a in AXES]
    chunks = nx // chunk

    def device(i):
        return tuple(
            lax.rem(m + v + n, n) if v else m for m, v, n in zip(me, VELOCITIES[i], sizes)
        )

    barrier = pltpu.get_barrier_semaphore()
    for i in range(1, 19):
        pl.semaphore_signal(barrier, inc=1, device_id=device(i), device_id_type=MESH_ID)

    def ck_copy(c):
        span = pl.ds(c * chunk, chunk)
        return pltpu.make_async_copy(ck_hbm.at[:, span], ck.at[:, span], ck_sem.at[c])

    def adj_copy(j):
        return pltpu.make_async_copy(
            adj_hbm.at[j], post.at[ADJ, SLOT[OPPOSITE[j]], pl.ds(1, nx)], adj_sem.at[j]
        )

    smalls = [
        pltpu.make_async_copy(por_hbm, por, small_sem.at[0]),
        pltpu.make_async_copy(sol_hbm, sol, small_sem.at[1]),
        pltpu.make_async_copy(gin_hbm, gin, small_sem.at[2]),
    ]
    smalls[0].start()
    smalls[1].start()
    for c in range(chunks):
        ck_copy(c).start()
    for j in range(19):
        adj_copy(j).start()
    smalls[2].start()

    def message(r, i):
        ex, ey, ez = VELOCITIES[i]
        if ez:
            d = side(ez)
            src, dst = zstage.at[r, d], zrecv.at[r, d, Z_GROUP[d].index(i)]
        elif ey and ex:
            d = side(ey)
            k = Y_GROUP[d].index(i)
            src = ystage.at[r, d, k, nx - 1 if ex > 0 else 0]
            dst = yhalo.at[r, d, k, 0 if ex > 0 else nx + 1]
        elif ey:
            d = side(ey)
            src, dst = ystage.at[r, d], yhalo.at[r, d, :, pl.ds(1, nx)]
        else:
            group = pl.ds(5 * side(ex), 5)
            src = post.at[r, group, nx if ex > 0 else 1]
            dst = post.at[r, group, 0 if ex > 0 else nx + 1]
        return pltpu.make_async_remote_copy(
            src_ref=src, dst_ref=dst, send_sem=send_sem.at[r, i], recv_sem=recv_sem.at[r, i],
            device_id=device(i), device_id_type=MESH_ID,
        )

    lane = lax.broadcasted_iota(jnp.int32, (ny, nz), 1)
    row = lax.broadcasted_iota(jnp.int32, (ny, nz), 0)
    lane_in = lax.rem(lane, nx)

    def stage(r, x, v, packed):
        result = []
        for d in range(2):
            edge = ny - 1 if d == 0 else 0
            for k, i in enumerate(Y_GROUP[d]):
                ystage[r, d, k, x] = v(i)[edge : edge + 1]
            total = None
            for k, i in enumerate(Z_GROUP[d]):
                turn = (k * nx + (1 if d == 0 else 0)) % nz
                moved = pltpu.roll(v(i), turn, 1) if turn else v(i)
                total = moved if total is None else jnp.where(lane < k * nx, total, moved)
            total = pltpu.roll(total, x, 1)
            result.append(jnp.where(lane_in == x, total, packed[d]))
        return tuple(result)

    def send(r, packed):
        for d in range(2):
            zstage[r, d] = packed[d]
        for i in range(1, 19):
            message(r, i).start()

    def receive(r):
        for i in range(1, 19):
            message(r, i).wait_recv()
        for d in range(2):
            face = zrecv[r, d, 0]
            merged = face
            for k, i in enumerate(Z_GROUP[d]):
                if k == 0:
                    continue
                ex, ey, _ = VELOCITIES[i]
                other = zrecv[r, d, k]
                if ex > 0:
                    part = jnp.where(
                        lane_in == 0, pltpu.roll(other, nz - (nx - 1), 1), pltpu.roll(face, 1, 1)
                    )
                elif ex < 0:
                    part = jnp.where(
                        lane_in == nx - 1, pltpu.roll(other, nx - 1, 1), pltpu.roll(face, nz - 1, 1)
                    )
                elif ey > 0:
                    part = jnp.where(row == 0, pltpu.roll(other, 1, 0), pltpu.roll(face, 1, 0))
                else:
                    part = jnp.where(
                        row == ny - 1, pltpu.roll(other, ny - 1, 0), pltpu.roll(face, ny - 1, 0)
                    )
                merged = jnp.where(lane // nx == k, part, merged)
            zmerge[r, d] = merged

    def streamed(r, x):
        turned = [pltpu.roll(zmerge[r, d], lax.rem(nz - x, nz), 1) for d in range(2)]
        f = []
        for i in range(19):
            ex, ey, ez = VELOCITIES[i]
            v = post[r, SLOT[i], x + 1 - ex]
            if ey:
                d = side(ey)
                halo = yhalo[r, d, Y_GROUP[d].index(i), x + 1 - ex]
                v = jnp.where(
                    row == (0 if ey > 0 else ny - 1),
                    jnp.broadcast_to(halo, (ny, nz)),
                    pltpu.roll(v, 1 if ey > 0 else ny - 1, 0),
                )
            if ez:
                d = side(ez)
                k = Z_GROUP[d].index(i)
                target = 0 if ez > 0 else nz - 1
                turn = (target - k * nx) % nz
                halo = pltpu.roll(turned[d], turn, 1) if turn else turned[d]
                v = jnp.where(
                    lane == target, halo, pltpu.roll(v, 1 if ez > 0 else nz - 1, 1)
                )
            f.append(v)
        return f

    def gamma_at(x):
        return jnp.where(sol[x] == 1, 1.0, por[x])

    zero = jnp.zeros((ny, nz), jnp.float32)

    def forward(r, f, x, packed):
        out = collide(f, gamma_at(x))
        for i in range(19):
            post[r, SLOT[i], x + 1] = out[i]
        return stage(r, x, lambda i: out[i], packed)

    smalls[0].wait()
    smalls[1].wait()

    def first(c, packed):
        ck_copy(c).wait()

        def plane(x, packed):
            return forward(0, [ck[i, x] for i in range(19)], x, packed)

        return lax.fori_loop(c * chunk, (c + 1) * chunk, plane, packed)

    packed = lax.fori_loop(0, chunks, first, (zero, zero))
    pl.semaphore_wait(barrier, 18)
    send(0, packed)

    for j in range(19):
        adj_copy(j).wait()
    packed = lax.fori_loop(
        0, nx, lambda x, p: stage(ADJ, x, lambda i: post[ADJ, SLOT[i], x + 1], p), (zero, zero)
    )
    send(ADJ, packed)

    for r in range(1, RECOMP):
        receive(r - 1)
        packed = lax.fori_loop(
            0, nx, lambda x, p, r=r: forward(r, streamed(r - 1, x), x, p), (zero, zero)
        )
        send(r, packed)

    receive(ADJ)

    def pull(x, carry):
        h = streamed(ADJ, x)
        g = [h[OPPOSITE[i]] for i in range(19)]
        gamma = gamma_at(x)
        keep = (1.0 - RELAX) * (1.0 - gamma)
        w = [WEIGHTS[0] * g[0]] + [None] * 18
        g0 = WEIGHTS[0] * g[0]
        g1 = [None] * 3
        g2 = {}
        base[0, x] = (keep + gamma) * g[0]
        coef[0, x] = RELAX * g[0]
        for i, o in PAIRS:
            plus = WEIGHTS[i] * (g[i] + g[o])
            minus = WEIGHTS[i] * (g[i] - g[o])
            g0 = g0 + plus
            v = VELOCITIES[i]
            for a in range(3):
                if v[a]:
                    term = minus if v[a] > 0 else -minus
                    g1[a] = term if g1[a] is None else g1[a] + term
                for b in range(a, 3):
                    if v[a] * v[b]:
                        term = plus if v[a] * v[b] > 0 else -plus
                        g2[a, b] = term if (a, b) not in g2 else g2[a, b] + term
            base[i, x] = keep * g[i] + gamma * g[o]
            base[o, x] = keep * g[o] + gamma * g[i]
            coef[i, x] = g[o] + (RELAX - 1.0) * g[i]
            coef[o, x] = g[i] + (RELAX - 1.0) * g[o]
        gsum[0, x] = g0
        for a in range(3):
            gsum[1 + a, x] = g1[a]
        for n, key in enumerate([(0, 0), (1, 1), (2, 2), (0, 1), (0, 2), (1, 2)]):
            gsum[4 + n, x] = g2[key]
        return carry

    lax.fori_loop(0, nx, pull, 0)
    smalls[2].wait()
    last = RECOMP - 1
    receive(last)

    def out_copy(c):
        span = pl.ds(c * chunk, chunk)
        return pltpu.make_async_copy(outv.at[:, span], out_hbm.at[:, span], out_sem.at[c])

    def final(x, carry):
        f = streamed(last, x)
        rho, flow = moments(f)
        inv = 1.0 / rho
        u = [j * inv for j in flow]
        g0 = gsum[0, x]
        g1 = [gsum[1 + a, x] for a in range(3)]
        xx, yy, zz, xy, xz, yz = [gsum[4 + n, x] for n in range(6)]
        gu = [
            xx * u[0] + xy * u[1] + xz * u[2],
            xy * u[0] + yy * u[1] + yz * u[2],
            xz * u[0] + yz * u[1] + zz * u[2],
        ]
        squared = u[0] * u[0] + u[1] * u[1] + u[2] * u[2]
        quad = 4.5 * (u[0] * gu[0] + u[1] * gu[1] + u[2] * gu[2]) - 1.5 * g0 * squared
        gain = RELAX * (1.0 - gamma_at(x))
        slope = gain * (g0 - quad)
        vec = [gain * (3.0 * g1[a] + 9.0 * gu[a] - 3.0 * g0 * u[a]) for a in range(3)]
        total = f[0] * coef[0, x]
        for i in range(1, 19):
            total = total + f[i] * coef[i, x]
        g1j = g1[0] * flow[0] + g1[1] * flow[1] + g1[2] * flow[2]
        total = total - RELAX * (rho * (g0 + quad) + 3.0 * g1j)
        pore = 1.0 - sol[x].astype(jnp.float32)
        gradv[x] = gin[x] + pore * total
        outv[0, x] = base[0, x] + slope
        for i, o in PAIRS:
            q = along(vec, i)
            outv[i, x] = base[i, x] + (slope + q)
            outv[o, x] = base[o, x] + (slope - q)
        return carry

    def finish(c, carry):
        lax.fori_loop(c * chunk, (c + 1) * chunk, final, 0)
        out_copy(c).start()
        return carry

    lax.fori_loop(0, chunks, finish, 0)
    grad_copy = pltpu.make_async_copy(gradv, grad_hbm, small_sem.at[3])
    grad_copy.start()
    for r in range(ROUNDS):
        for i in range(1, 19):
            message(r, i).wait_send()
    for c in range(chunks):
        out_copy(c).wait()
    grad_copy.wait()


def body(checkpoint, adjoint, porosity, solid, gradient_in):
    _, nx, ny, nz = checkpoint.shape
    chunk = 4 if nx % 4 == 0 else 1
    chunks = nx // chunk
    f32 = jnp.float32
    block = (nx, ny, nz)
    vm = pltpu.VMEM
    dma = pltpu.SemaphoreType.DMA
    return pl.pallas_call(
        functools.partial(kernel, nx, ny, nz, chunk),
        out_shape=(
            jax.ShapeDtypeStruct((19,) + block, f32),
            jax.ShapeDtypeStruct(block, f32),
        ),
        in_specs=[pl.BlockSpec(memory_space=pl.ANY)] * 5,
        out_specs=(pl.BlockSpec(memory_space=pl.ANY),) * 2,
        scratch_shapes=[
            vm((19,) + block, f32),
            vm((ROUNDS, 19, nx + 2, ny, nz), f32),
            vm((ROUNDS, 2, 5, nx, 1, nz), f32),
            vm((ROUNDS, 2, 5, nx + 2, 1, nz), f32),
            vm((ROUNDS, 2, ny, nz), f32),
            vm((ROUNDS, 2, 5, ny, nz), f32),
            vm((ROUNDS, 2, ny, nz), f32),
            vm((19,) + block, f32),
            vm((19,) + block, f32),
            vm((10,) + block, f32),
            vm(block, f32),
            vm(block, jnp.int32),
            vm(block, f32),
            vm((19,) + block, f32),
            vm(block, f32),
            dma((ROUNDS, 19)),
            dma((ROUNDS, 19)),
            dma((chunks,)),
            dma((19,)),
            dma((4,)),
            dma((chunks,)),
        ],
        compiler_params=pltpu.CompilerParams(
            collective_id=0, has_side_effects=True, vmem_limit_bytes=48 * 1024 * 1024
        ),
    )(checkpoint, adjoint, porosity, solid, gradient_in)


def solution(mesh):
    in_specs = (
        P(None, "gx", "gy", "gz"),
        P(None, "gx", "gy", "gz"),
        P("gx", "gy", "gz"),
        P("gx", "gy", "gz"),
        P("gx", "gy", "gz"),
    )
    out_specs = (P(None, "gx", "gy", "gz"), P("gx", "gy", "gz"))
    return jax.shard_map(body, mesh=mesh, in_specs=in_specs, out_specs=out_specs, check_vma=False)
```

```python
import functools

import jax
import jax.numpy as jnp
from jax import lax
from jax.experimental import pallas as pl
from jax.experimental.pallas import tpu as pltpu
from jax.sharding import PartitionSpec as P

RECOMP = 3
VELOCITIES = [
    (0, 0, 0),
    (1, 0, 0),
    (-1, 0, 0),
    (0, 1, 0),
    (0, -1, 0),
    (0, 0, 1),
    (0, 0, -1),
    (1, 1, 0),
    (-1, -1, 0),
    (1, -1, 0),
    (-1, 1, 0),
    (1, 0, 1),
    (-1, 0, -1),
    (1, 0, -1),
    (-1, 0, 1),
    (0, 1, 1),
    (0, -1, -1),
    (0, 1, -1),
    (0, -1, 1),
]
OPPOSITE = [0, 2, 1, 4, 3, 6, 5, 8, 7, 10, 9, 12, 11, 14, 13, 16, 15, 18, 17]
PAIRS = [(1, 2), (3, 4), (5, 6), (7, 8), (9, 10), (11, 12), (13, 14), (15, 16), (17, 18)]
WEIGHTS = [1.0 / 3.0] + [1.0 / 18.0] * 6 + [1.0 / 36.0] * 12
RELAX = 1.25

ORDER = [1, 7, 9, 11, 13, 2, 8, 10, 12, 14, 0, 3, 4, 5, 6, 15, 16, 17, 18]
SLOT = [ORDER.index(i) for i in range(19)]
Y_GROUP = [[i for i in range(19) if VELOCITIES[i][1] == s] for s in (1, -1)]
Z_GROUP = [[i for i in range(19) if VELOCITIES[i][2] == s] for s in (1, -1)]
AXES = ("gx", "gy", "gz")
ADJ = RECOMP
ROUNDS = RECOMP + 1
MESH_ID = pl.DeviceIdType.MESH


def side(component):
    return 0 if component > 0 else 1


def moments(f):
    plus = [f[i] + f[o] for i, o in PAIRS]
    minus = [f[i] - f[o] for i, o in PAIRS]
    rho = f[0]
    for s in plus:
        rho = rho + s
    flow = []
    for axis in range(3):
        total = None
        for (i, _), d in zip(PAIRS, minus):
            c = VELOCITIES[i][axis]
            if c == 0:
                continue
            total = d if total is None else (total + d if c > 0 else total - d)
        flow.append(total)
    return rho, flow


def along(vector, i):
    total = None
    for axis in range(3):
        c = VELOCITIES[i][axis]
        if c == 0:
            continue
        if total is None:
            total = vector[axis] if c > 0 else -vector[axis]
        else:
            total = total + vector[axis] if c > 0 else total - vector[axis]
    return total


def collide(f, gamma):
    rho, flow = moments(f)
    inv = 1.0 / rho
    u = [j * inv for j in flow]
    fluid = 1.0 - gamma
    keep = (1.0 - RELAX) * fluid
    gain = RELAX * fluid
    scaled = gain * rho
    squared = u[0] * u[0] + u[1] * u[1] + u[2] * u[2]
    base = scaled - 1.5 * scaled * squared
    triple = (3.0 / 36.0) * scaled
    base_edge = (1.0 / 36.0) * base
    base_face = base_edge + base_edge
    post = [None] * 19
    post[0] = (keep + gamma) * f[0] + (1.0 / 3.0) * base
    for i, o in PAIRS:
        q = along(u, i)
        t = triple * q
        even = 1.5 * q * t
        if i < 7:
            t = t + t
            even = even + even + base_face
        else:
            even = even + base_edge
        post[i] = keep * f[i] + gamma * f[o] + (even + t)
        post[o] = keep * f[o] + gamma * f[i] + (even - t)
    return post


def kernel(nx, ny, nz, chunk, ck_hbm, adj_hbm, por_hbm, sol_hbm, gin_hbm, outv, gradv,
           ck, post, ystage, yhalo, zstage, zrecv, base, coef, gsum, por, sol, gin,
           send_sem, recv_sem, ck_sem, adj_sem, small_sem):
    sizes = [lax.axis_size(a) for a in AXES]
    me = [lax.axis_index(a) for a in AXES]
    chunks = nx // chunk

    def device(i):
        return tuple(
            lax.rem(m + v + n, n) if v else m for m, v, n in zip(me, VELOCITIES[i], sizes)
        )

    barrier = pltpu.get_barrier_semaphore()
    for i in range(1, 19):
        pl.semaphore_signal(barrier, inc=1, device_id=device(i), device_id_type=MESH_ID)

    def ck_copy(c):
        span = pl.ds(c * chunk, chunk)
        return pltpu.make_async_copy(ck_hbm.at[:, span], ck.at[:, span], ck_sem.at[c])

    def adj_copy(j):
        return pltpu.make_async_copy(
            adj_hbm.at[j], post.at[ADJ, SLOT[OPPOSITE[j]], pl.ds(1, nx)], adj_sem.at[j]
        )

    smalls = [
        pltpu.make_async_copy(por_hbm, por, small_sem.at[0]),
        pltpu.make_async_copy(sol_hbm, sol, small_sem.at[1]),
        pltpu.make_async_copy(gin_hbm, gin, small_sem.at[2]),
    ]
    smalls[0].start()
    smalls[1].start()
    for c in range(chunks):
        ck_copy(c).start()

    def message(r, i):
        ex, ey, ez = VELOCITIES[i]
        if ez:
            d = side(ez)
            src, dst = zstage.at[r, d], zrecv.at[r, d, Z_GROUP[d].index(i)]
        elif ey and ex:
            d = side(ey)
            k = Y_GROUP[d].index(i)
            src = ystage.at[r, d, k, nx - 1 if ex > 0 else 0]
            dst = yhalo.at[r, d, k, 0 if ex > 0 else nx + 1]
        elif ey:
            d = side(ey)
            src, dst = ystage.at[r, d], yhalo.at[r, d, :, pl.ds(1, nx)]
        else:
            group = pl.ds(5 * side(ex), 5)
            src = post.at[r, group, nx if ex > 0 else 1]
            dst = post.at[r, group, 0 if ex > 0 else nx + 1]
        return pltpu.make_async_remote_copy(
            src_ref=src, dst_ref=dst, send_sem=send_sem.at[r, i], recv_sem=recv_sem.at[r, i],
            device_id=device(i), device_id_type=MESH_ID,
        )

    lane = lax.broadcasted_iota(jnp.int32, (ny, nz), 1)
    row = lax.broadcasted_iota(jnp.int32, (ny, nz), 0)

    def turned(i, x, v):
        ez = VELOCITIES[i][2]
        if ez == 0:
            return v
        k = Z_GROUP[side(ez)].index(i) * nx + x
        return pltpu.roll(v, k + 1 if ez > 0 else k, 1)

    def stage(r, x, v, packed):
        result = []
        for d in range(2):
            edge = ny - 1 if d == 0 else 0
            for k, i in enumerate(Y_GROUP[d]):
                ystage[r, d, k, x] = v[i][edge : edge + 1]
            total = packed[d]
            for k, i in enumerate(Z_GROUP[d]):
                total = jnp.where(lane == k * nx + x, v[i], total)
            result.append(total)
        return tuple(result)

    def send(r, packed):
        for d in range(2):
            zstage[r, d] = packed[d]
        for i in range(1, 19):
            message(r, i).start()

    def receive(r):
        for i in range(1, 19):
            message(r, i).wait_recv()

    def streamed(r, x):
        f = []
        for i in range(19):
            ex, ey, ez = VELOCITIES[i]
            v = post[r, SLOT[i], x + 1 - ex]
            if ez:
                d = side(ez)
                n = Z_GROUP[d].index(i)
                at = lax.rem(x - ex + nx, nx) if ex else x
                k = n * nx + at
                outer = (nx - x) // nx if ex > 0 else (x + 1) // nx if ex < 0 else 0
                v = jnp.where(lane == k, zrecv[r, d, n * outer], v)
            if ey:
                e = side(ey)
                halo = yhalo[r, e, Y_GROUP[e].index(i), x + 1 - ex]
                if ez:
                    edge = ny - 1 if ey > 0 else 0
                    halo = jnp.where(lane[:1] == k, zrecv[r, d, n, edge : edge + 1], halo)
                v = jnp.where(
                    row == (0 if ey > 0 else ny - 1),
                    jnp.broadcast_to(halo, (ny, nz)),
                    pltpu.roll(v, 1 if ey > 0 else ny - 1, 0),
                )
            if ez:
                v = pltpu.roll(v, lax.rem(nz - k, nz) if ez > 0 else nz - 1 - k, 1)
            f.append(v)
        return f

    def gamma_at(x):
        return jnp.where(sol[x] == 1, 1.0, por[x])

    zero = jnp.zeros((ny, nz), jnp.float32)

    def forward(r, f, x, packed):
        out = [turned(i, x, v) for i, v in enumerate(collide(f, gamma_at(x)))]
        for i in range(19):
            post[r, SLOT[i], x + 1] = out[i]
        return stage(r, x, out, packed)

    def lift(x, packed):
        out = [turned(i, x, post[ADJ, SLOT[i], x + 1]) for i in range(19)]
        for i in Z_GROUP[0] + Z_GROUP[1]:
            post[ADJ, SLOT[i], x + 1] = out[i]
        return stage(ADJ, x, out, packed)

    smalls[0].wait()
    smalls[1].wait()

    def first(c, packed):
        ck_copy(c).wait()

        def plane(x, packed):
            return forward(0, [ck[i, x] for i in range(19)], x, packed)

        return lax.fori_loop(c * chunk, (c + 1) * chunk, plane, packed)

    packed = lax.fori_loop(0, chunks // 2, first, (zero, zero))
    for j in range(19):
        adj_copy(j).start()
    smalls[2].start()
    packed = lax.fori_loop(chunks // 2, chunks, first, packed)
    pl.semaphore_wait(barrier, 18)
    send(0, packed)

    for j in range(19):
        adj_copy(j).wait()
    packed = lax.fori_loop(0, nx, lift, (zero, zero), unroll=4)
    send(ADJ, packed)

    for r in range(1, RECOMP):
        receive(r - 1)
        packed = lax.fori_loop(
            0, nx, lambda x, p, r=r: forward(r, streamed(r - 1, x), x, p), (zero, zero), unroll=4
        )
        send(r, packed)

    receive(ADJ)

    def pull(x, carry):
        h = streamed(ADJ, x)
        g = [h[OPPOSITE[i]] for i in range(19)]
        gamma = gamma_at(x)
        keep = (1.0 - RELAX) * (1.0 - gamma)
        w = [WEIGHTS[0] * g[0]] + [None] * 18
        g0 = WEIGHTS[0] * g[0]
        g1 = [None] * 3
        g2 = {}
        base[0, x] = (keep + gamma) * g[0]
        coef[0, x] = RELAX * g[0]
        for i, o in PAIRS:
            plus = WEIGHTS[i] * (g[i] + g[o])
            minus = WEIGHTS[i] * (g[i] - g[o])
            g0 = g0 + plus
            v = VELOCITIES[i]
            for a in range(3):
                if v[a]:
                    term = minus if v[a] > 0 else -minus
                    g1[a] = term if g1[a] is None else g1[a] + term
                for b in range(a, 3):
                    if v[a] * v[b]:
                        term = plus if v[a] * v[b] > 0 else -plus
                        g2[a, b] = term if (a, b) not in g2 else g2[a, b] + term
            base[i, x] = keep * g[i] + gamma * g[o]
            base[o, x] = keep * g[o] + gamma * g[i]
            coef[i, x] = g[o] + (RELAX - 1.0) * g[i]
            coef[o, x] = g[i] + (RELAX - 1.0) * g[o]
        gsum[0, x] = g0
        for a in range(3):
            gsum[1 + a, x] = g1[a]
        for n, key in enumerate([(0, 0), (1, 1), (2, 2), (0, 1), (0, 2), (1, 2)]):
            gsum[4 + n, x] = g2[key]
        return carry

    lax.fori_loop(0, nx, pull, 0, unroll=4)
    smalls[2].wait()
    last = RECOMP - 1
    receive(last)

    def final(x, carry):
        f = streamed(last, x)
        rho, flow = moments(f)
        inv = 1.0 / rho
        u = [j * inv for j in flow]
        g0 = gsum[0, x]
        g1 = [gsum[1 + a, x] for a in range(3)]
        xx, yy, zz, xy, xz, yz = [gsum[4 + n, x] for n in range(6)]
        gu = [
            xx * u[0] + xy * u[1] + xz * u[2],
            xy * u[0] + yy * u[1] + yz * u[2],
            xz * u[0] + yz * u[1] + zz * u[2],
        ]
        squared = u[0] * u[0] + u[1] * u[1] + u[2] * u[2]
        quad = 4.5 * (u[0] * gu[0] + u[1] * gu[1] + u[2] * gu[2]) - 1.5 * g0 * squared
        gain = RELAX * (1.0 - gamma_at(x))
        slope = gain * (g0 - quad)
        vec = [gain * (3.0 * g1[a] + 9.0 * gu[a] - 3.0 * g0 * u[a]) for a in range(3)]
        total = f[0] * coef[0, x]
        for i in range(1, 19):
            total = total + f[i] * coef[i, x]
        g1j = g1[0] * flow[0] + g1[1] * flow[1] + g1[2] * flow[2]
        total = total - RELAX * (rho * (g0 + quad) + 3.0 * g1j)
        pore = 1.0 - sol[x].astype(jnp.float32)
        gradv[x] = gin[x] + pore * total
        outv[0, x] = base[0, x] + slope
        for i, o in PAIRS:
            q = along(vec, i)
            outv[i, x] = base[i, x] + (slope + q)
            outv[o, x] = base[o, x] + (slope - q)
        return carry

    lax.fori_loop(0, nx, final, 0, unroll=4)
    for r in range(ROUNDS):
        for i in range(1, 19):
            message(r, i).wait_send()


def body(checkpoint, adjoint, porosity, solid, gradient_in):
    _, nx, ny, nz = checkpoint.shape
    chunk = 4 if nx % 4 == 0 else 1
    chunks = nx // chunk
    f32 = jnp.float32
    block = (nx, ny, nz)
    vm = pltpu.VMEM
    dma = pltpu.SemaphoreType.DMA
    return pl.pallas_call(
        functools.partial(kernel, nx, ny, nz, chunk),
        out_shape=(
            jax.ShapeDtypeStruct((19,) + block, f32),
            jax.ShapeDtypeStruct(block, f32),
        ),
        in_specs=[pl.BlockSpec(memory_space=pltpu.HBM)] * 5,
        out_specs=(pl.BlockSpec(memory_space=pltpu.VMEM),) * 2,
        scratch_shapes=[
            vm((19,) + block, f32),
            vm((ROUNDS, 19, nx + 2, ny, nz), f32),
            vm((ROUNDS, 2, 5, nx, 1, nz), f32),
            vm((ROUNDS, 2, 5, nx + 2, 1, nz), f32),
            vm((ROUNDS, 2, ny, nz), f32),
            vm((ROUNDS, 2, 5, ny, nz), f32),
            vm((19,) + block, f32),
            vm((19,) + block, f32),
            vm((10,) + block, f32),
            vm(block, f32),
            vm(block, jnp.int32),
            vm(block, f32),
            dma((ROUNDS, 19)),
            dma((ROUNDS, 19)),
            dma((chunks,)),
            dma((19,)),
            dma((3,)),
        ],
        compiler_params=pltpu.CompilerParams(
            collective_id=0, has_side_effects=True, vmem_limit_bytes=62 * 1024 * 1024
        ),
    )(checkpoint, adjoint, porosity, solid, gradient_in)


def solution(mesh):
    in_specs = (
        P(None, "gx", "gy", "gz"),
        P(None, "gx", "gy", "gz"),
        P("gx", "gy", "gz"),
        P("gx", "gy", "gz"),
        P("gx", "gy", "gz"),
    )
    out_specs = (P(None, "gx", "gy", "gz"), P("gx", "gy", "gz"))
    return jax.shard_map(body, mesh=mesh, in_specs=in_specs, out_specs=out_specs, check_vma=False)
```

```python
import functools

import jax
import jax.numpy as jnp
from jax import lax
from jax.experimental import pallas as pl
from jax.experimental.pallas import tpu as pltpu
from jax.sharding import PartitionSpec as P

RECOMP = 3
VELOCITIES = [
    (0, 0, 0),
    (1, 0, 0),
    (-1, 0, 0),
    (0, 1, 0),
    (0, -1, 0),
    (0, 0, 1),
    (0, 0, -1),
    (1, 1, 0),
    (-1, -1, 0),
    (1, -1, 0),
    (-1, 1, 0),
    (1, 0, 1),
    (-1, 0, -1),
    (1, 0, -1),
    (-1, 0, 1),
    (0, 1, 1),
    (0, -1, -1),
    (0, 1, -1),
    (0, -1, 1),
]
OPPOSITE = [0, 2, 1, 4, 3, 6, 5, 8, 7, 10, 9, 12, 11, 14, 13, 16, 15, 18, 17]
PAIRS = [(1, 2), (3, 4), (5, 6), (7, 8), (9, 10), (11, 12), (13, 14), (15, 16), (17, 18)]
WEIGHTS = [1.0 / 3.0] + [1.0 / 18.0] * 6 + [1.0 / 36.0] * 12
RELAX = 1.25

ORDER = [1, 7, 9, 11, 13, 2, 8, 10, 12, 14, 0, 3, 4, 5, 6, 15, 16, 17, 18]
SLOT = [ORDER.index(i) for i in range(19)]
Y_GROUP = [[i for i in range(19) if VELOCITIES[i][1] == s] for s in (1, -1)]
Z_GROUP = [[i for i in range(19) if VELOCITIES[i][2] == s] for s in (1, -1)]
X_MESSAGES = [i for i in range(1, 19) if VELOCITIES[i][0]]
REST_MESSAGES = [i for i in range(1, 19) if not VELOCITIES[i][0]]
AXES = ("gx", "gy", "gz")
ADJ = RECOMP
ROUNDS = RECOMP + 1
MESH_ID = pl.DeviceIdType.MESH


def side(component):
    return 0 if component > 0 else 1


def moments(f):
    plus = [f[i] + f[o] for i, o in PAIRS]
    minus = [f[i] - f[o] for i, o in PAIRS]
    rho = f[0]
    for s in plus:
        rho = rho + s
    flow = []
    for axis in range(3):
        total = None
        for (i, _), d in zip(PAIRS, minus):
            c = VELOCITIES[i][axis]
            if c == 0:
                continue
            total = d if total is None else (total + d if c > 0 else total - d)
        flow.append(total)
    return rho, flow


def along(vector, i):
    total = None
    for axis in range(3):
        c = VELOCITIES[i][axis]
        if c == 0:
            continue
        if total is None:
            total = vector[axis] if c > 0 else -vector[axis]
        else:
            total = total + vector[axis] if c > 0 else total - vector[axis]
    return total


def collide(f, gamma):
    rho, flow = moments(f)
    inv = 1.0 / rho
    u = [j * inv for j in flow]
    fluid = 1.0 - gamma
    keep = (1.0 - RELAX) * fluid
    gain = RELAX * fluid
    scaled = gain * rho
    squared = u[0] * u[0] + u[1] * u[1] + u[2] * u[2]
    base = scaled - 1.5 * scaled * squared
    triple = (3.0 / 36.0) * scaled
    base_edge = (1.0 / 36.0) * base
    base_face = base_edge + base_edge
    post = [None] * 19
    post[0] = (keep + gamma) * f[0] + (1.0 / 3.0) * base
    for i, o in PAIRS:
        q = along(u, i)
        t = triple * q
        even = 1.5 * q * t
        if i < 7:
            t = t + t
            even = even + even + base_face
        else:
            even = even + base_edge
        post[i] = keep * f[i] + gamma * f[o] + (even + t)
        post[o] = keep * f[o] + gamma * f[i] + (even - t)
    return post


def kernel(nx, ny, nz, ck_hbm, adj_hbm, por_hbm, sol_hbm, gin_hbm, outv, gradv,
           ck, post, ystage, yhalo, zstage, zedge, zrecv, base, coef, gsum, por, sol, gin,
           send_sem, recv_sem, ck_sem, adj_sem, small_sem):
    sizes = [lax.axis_size(a) for a in AXES]
    me = [lax.axis_index(a) for a in AXES]

    def device(i):
        return tuple(
            lax.rem(m + v + n, n) if v else m for m, v, n in zip(me, VELOCITIES[i], sizes)
        )

    barrier = pltpu.get_barrier_semaphore()
    for i in range(1, 19):
        pl.semaphore_signal(barrier, inc=1, device_id=device(i), device_id_type=MESH_ID)

    half = nx // 2
    spans = [(0, 1), (nx - 1, 1), (1, half - 1), (half, nx - 1 - half)]

    def ck_copy(c):
        span = pl.ds(*spans[c])
        return pltpu.make_async_copy(ck_hbm.at[:, span], ck.at[:, span], ck_sem.at[c])

    def adj_copy(j):
        return pltpu.make_async_copy(
            adj_hbm.at[j], post.at[ADJ, SLOT[OPPOSITE[j]], pl.ds(1, nx)], adj_sem.at[j]
        )

    smalls = [
        pltpu.make_async_copy(por_hbm, por, small_sem.at[0]),
        pltpu.make_async_copy(sol_hbm, sol, small_sem.at[1]),
        pltpu.make_async_copy(gin_hbm, gin, small_sem.at[2]),
    ]
    smalls[0].start()
    smalls[1].start()
    for c in range(4):
        ck_copy(c).start()

    def message(r, i):
        ex, ey, ez = VELOCITIES[i]
        if ez:
            d = side(ez)
            src = zedge.at[r, d] if ex else zstage.at[r, d]
            dst = zrecv.at[r, d, Z_GROUP[d].index(i)]
        elif ey and ex:
            d = side(ey)
            k = Y_GROUP[d].index(i)
            src = ystage.at[r, d, k, nx - 1 if ex > 0 else 0]
            dst = yhalo.at[r, d, k, 0 if ex > 0 else nx + 1]
        elif ey:
            d = side(ey)
            src, dst = ystage.at[r, d], yhalo.at[r, d, :, pl.ds(1, nx)]
        else:
            group = pl.ds(5 * side(ex), 5)
            src = post.at[r, group, nx if ex > 0 else 1]
            dst = post.at[r, group, 0 if ex > 0 else nx + 1]
        return pltpu.make_async_remote_copy(
            src_ref=src, dst_ref=dst, send_sem=send_sem.at[r, i], recv_sem=recv_sem.at[r, i],
            device_id=device(i), device_id_type=MESH_ID,
        )

    lane = lax.broadcasted_iota(jnp.int32, (ny, nz), 1)
    row = lax.broadcasted_iota(jnp.int32, (ny, nz), 0)

    def turned(i, x, v):
        ez = VELOCITIES[i][2]
        if ez == 0:
            return v
        k = Z_GROUP[side(ez)].index(i) * nx + x
        return pltpu.roll(v, k + 1 if ez > 0 else k, 1)

    def stage(r, x, v, packed):
        result = []
        for d in range(2):
            edge = ny - 1 if d == 0 else 0
            for k, i in enumerate(Y_GROUP[d]):
                ystage[r, d, k, x] = v[i][edge : edge + 1]
            total = packed[d]
            for k, i in enumerate(Z_GROUP[d]):
                total = jnp.where(lane == k * nx + x, v[i], total)
            result.append(total)
        return tuple(result)

    def send_x(r, packed):
        for d in range(2):
            zedge[r, d] = packed[d]
        for i in X_MESSAGES:
            message(r, i).start()

    def send_rest(r, packed):
        for d in range(2):
            zstage[r, d] = packed[d]
        for i in REST_MESSAGES:
            message(r, i).start()

    def receive(r):
        for i in range(1, 19):
            message(r, i).wait_recv()

    def streamed(r, x):
        f = []
        for i in range(19):
            ex, ey, ez = VELOCITIES[i]
            v = post[r, SLOT[i], x + 1 - ex]
            if ez:
                d = side(ez)
                n = Z_GROUP[d].index(i)
                at = lax.rem(x - ex + nx, nx) if ex else x
                k = n * nx + at
                outer = (nx - x) // nx if ex > 0 else (x + 1) // nx if ex < 0 else 0
                v = jnp.where(lane == k, zrecv[r, d, n * outer], v)
            if ey:
                e = side(ey)
                halo = yhalo[r, e, Y_GROUP[e].index(i), x + 1 - ex]
                if ez:
                    edge = ny - 1 if ey > 0 else 0
                    halo = jnp.where(lane[:1] == k, zrecv[r, d, n, edge : edge + 1], halo)
                v = jnp.where(
                    row == (0 if ey > 0 else ny - 1),
                    jnp.broadcast_to(halo, (ny, nz)),
                    pltpu.roll(v, 1 if ey > 0 else ny - 1, 0),
                )
            if ez:
                v = pltpu.roll(v, lax.rem(nz - k, nz) if ez > 0 else nz - 1 - k, 1)
            f.append(v)
        return f

    def gamma_at(x):
        return jnp.where(sol[x] == 1, 1.0, por[x])

    zero = jnp.zeros((ny, nz), jnp.float32)

    def forward(r, f, x, packed):
        out = [turned(i, x, v) for i, v in enumerate(collide(f, gamma_at(x)))]
        for i in range(19):
            post[r, SLOT[i], x + 1] = out[i]
        return stage(r, x, out, packed)

    def lift(x, packed):
        out = [turned(i, x, post[ADJ, SLOT[i], x + 1]) for i in range(19)]
        for i in Z_GROUP[0] + Z_GROUP[1]:
            post[ADJ, SLOT[i], x + 1] = out[i]
        return stage(ADJ, x, out, packed)

    smalls[0].wait()
    smalls[1].wait()

    def first(x, packed):
        return forward(0, [ck[i, x] for i in range(19)], x, packed)

    def edge_planes(step, packed):
        return lax.fori_loop(0, 2, lambda n, p: step(n * (nx - 1), p), packed, unroll=2)

    ck_copy(0).wait()
    ck_copy(1).wait()
    packed = edge_planes(first, (zero, zero))
    edge_packed = packed
    ck_copy(2).wait()
    for j in range(19):
        adj_copy(j).start()
    smalls[2].start()
    packed = lax.fori_loop(1, half, first, packed)
    pl.semaphore_wait(barrier, 18)
    send_x(0, edge_packed)
    ck_copy(3).wait()
    packed = lax.fori_loop(half, nx - 1, first, packed)
    send_rest(0, packed)

    for j in range(19):
        adj_copy(j).wait()
    packed = lax.fori_loop(0, nx, lift, (zero, zero), unroll=4)
    send_x(ADJ, packed)
    send_rest(ADJ, packed)

    for r in range(1, RECOMP):
        receive(r - 1)

        def step(x, p, r=r):
            return forward(r, streamed(r - 1, x), x, p)

        packed = edge_planes(step, (zero, zero))
        send_x(r, packed)
        packed = lax.fori_loop(1, nx - 1, step, packed, unroll=7)
        send_rest(r, packed)

    receive(ADJ)

    def pull(x, carry):
        h = streamed(ADJ, x)
        g = [h[OPPOSITE[i]] for i in range(19)]
        gamma = gamma_at(x)
        keep = (1.0 - RELAX) * (1.0 - gamma)
        w = [WEIGHTS[0] * g[0]] + [None] * 18
        g0 = WEIGHTS[0] * g[0]
        g1 = [None] * 3
        g2 = {}
        base[0, x] = (keep + gamma) * g[0]
        coef[0, x] = RELAX * g[0]
        for i, o in PAIRS:
            plus = WEIGHTS[i] * (g[i] + g[o])
            minus = WEIGHTS[i] * (g[i] - g[o])
            g0 = g0 + plus
            v = VELOCITIES[i]
            for a in range(3):
                if v[a]:
                    term = minus if v[a] > 0 else -minus
                    g1[a] = term if g1[a] is None else g1[a] + term
                for b in range(a, 3):
                    if v[a] * v[b]:
                        term = plus if v[a] * v[b] > 0 else -plus
                        g2[a, b] = term if (a, b) not in g2 else g2[a, b] + term
            base[i, x] = keep * g[i] + gamma * g[o]
            base[o, x] = keep * g[o] + gamma * g[i]
            coef[i, x] = g[o] + (RELAX - 1.0) * g[i]
            coef[o, x] = g[i] + (RELAX - 1.0) * g[o]
        gsum[0, x] = g0
        for a in range(3):
            gsum[1 + a, x] = g1[a]
        for n, key in enumerate([(0, 0), (1, 1), (2, 2), (0, 1), (0, 2), (1, 2)]):
            gsum[4 + n, x] = g2[key]
        return carry

    lax.fori_loop(0, nx, pull, 0, unroll=4)
    smalls[2].wait()
    last = RECOMP - 1
    receive(last)

    def final(x, carry):
        f = streamed(last, x)
        rho, flow = moments(f)
        inv = 1.0 / rho
        u = [j * inv for j in flow]
        g0 = gsum[0, x]
        g1 = [gsum[1 + a, x] for a in range(3)]
        xx, yy, zz, xy, xz, yz = [gsum[4 + n, x] for n in range(6)]
        gu = [
            xx * u[0] + xy * u[1] + xz * u[2],
            xy * u[0] + yy * u[1] + yz * u[2],
            xz * u[0] + yz * u[1] + zz * u[2],
        ]
        squared = u[0] * u[0] + u[1] * u[1] + u[2] * u[2]
        quad = 4.5 * (u[0] * gu[0] + u[1] * gu[1] + u[2] * gu[2]) - 1.5 * g0 * squared
        gain = RELAX * (1.0 - gamma_at(x))
        slope = gain * (g0 - quad)
        vec = [gain * (3.0 * g1[a] + 9.0 * gu[a] - 3.0 * g0 * u[a]) for a in range(3)]
        total = f[0] * coef[0, x]
        for i in range(1, 19):
            total = total + f[i] * coef[i, x]
        g1j = g1[0] * flow[0] + g1[1] * flow[1] + g1[2] * flow[2]
        total = total - RELAX * (rho * (g0 + quad) + 3.0 * g1j)
        pore = 1.0 - sol[x].astype(jnp.float32)
        gradv[x] = gin[x] + pore * total
        outv[0, x] = base[0, x] + slope
        for i, o in PAIRS:
            q = along(vec, i)
            outv[i, x] = base[i, x] + (slope + q)
            outv[o, x] = base[o, x] + (slope - q)
        return carry

    lax.fori_loop(0, nx, final, 0, unroll=4)
    for r in range(ROUNDS):
        for i in range(1, 19):
            message(r, i).wait_send()


def body(checkpoint, adjoint, porosity, solid, gradient_in):
    _, nx, ny, nz = checkpoint.shape
    f32 = jnp.float32
    block = (nx, ny, nz)
    vm = pltpu.VMEM
    dma = pltpu.SemaphoreType.DMA
    return pl.pallas_call(
        functools.partial(kernel, nx, ny, nz),
        out_shape=(
            jax.ShapeDtypeStruct((19,) + block, f32),
            jax.ShapeDtypeStruct(block, f32),
        ),
        in_specs=[pl.BlockSpec(memory_space=pltpu.HBM)] * 5,
        out_specs=(pl.BlockSpec(memory_space=pltpu.VMEM),) * 2,
        scratch_shapes=[
            vm((19,) + block, f32),
            vm((ROUNDS, 19, nx + 2, ny, nz), f32),
            vm((ROUNDS, 2, 5, nx, 1, nz), f32),
            vm((ROUNDS, 2, 5, nx + 2, 1, nz), f32),
            vm((ROUNDS, 2, ny, nz), f32),
            vm((ROUNDS, 2, ny, nz), f32),
            vm((ROUNDS, 2, 5, ny, nz), f32),
            vm((19,) + block, f32),
            vm((19,) + block, f32),
            vm((10,) + block, f32),
            vm(block, f32),
            vm(block, jnp.int32),
            vm(block, f32),
            dma((ROUNDS, 19)),
            dma((ROUNDS, 19)),
            dma((4,)),
            dma((19,)),
            dma((3,)),
        ],
        compiler_params=pltpu.CompilerParams(
            collective_id=0, has_side_effects=True, vmem_limit_bytes=62 * 1024 * 1024
        ),
    )(checkpoint, adjoint, porosity, solid, gradient_in)


def solution(mesh):
    in_specs = (
        P(None, "gx", "gy", "gz"),
        P(None, "gx", "gy", "gz"),
        P("gx", "gy", "gz"),
        P("gx", "gy", "gz"),
        P("gx", "gy", "gz"),
    )
    out_specs = (P(None, "gx", "gy", "gz"), P("gx", "gy", "gz"))
    return jax.shard_map(body, mesh=mesh, in_specs=in_specs, out_specs=out_specs, check_vma=False)
```
